128 devices in a mesh: chan: 8 (over y_hi, z), bin: 16 (over y_lo, x, core).
Axes of the slice: x: 4, y: 4 (y_hi: 2, y_lo: 2; y = y_hi * 2 + y_lo), z: 4, core: 2. Of those that a mesh axis runs over, the one named last changes fastest.
Arguments:
- spectra: bfloat16 [128, 2, 512, 2048], P('bin', None, None, 'chan')
- valid: int32 [16, 512], P('chan'), may hold values from 0 to 1, as said below
Outputs:
- stacked: bfloat16 [16, 9, 128, 2, 128, 128], P('chan', None, 'bin')
The draws below stay inside these ranges and needn't reach their ends.
Inputs may be any that keep to these rules, and one draw needn't show every extreme that they name: `valid`: each entry is 0 or 1; in every draw exactly one channel block, drawn from the seed, has no usable segment at all.
All inputs are finite; a program needn't handle non-finite values.
Results may differ from the reference program's by a relative error of at most 0.0043.
Values may be sent and summed in bfloat16 or wider, within the bound.
No kernel may reach another device: no remote copies, remote signals or barrier semaphores. Data moves between devices by JAX's collectives and lax.ppermute only.
A program may use at most 128 MiB of HBM per device.

```python
import jax
import jax.numpy as jnp
from jax import lax

BLOCK = 128
SEG = 512
NB = 16
NH = 9
CHANNELS = 2048
BINS = 128


def draw_spectra(key, part):
    key = jax.random.fold_in(key, 11)
    keys = jax.random.split(key, 5)
    source = jax.random.normal(keys[0], (BINS, 2, SEG, 1), jnp.float32)
    gains = jax.random.uniform(keys[1], (1, 1, 1, CHANNELS), jnp.float32, 0.3, 1.2)
    signs = jnp.where(jax.random.normal(keys[2], (1, 1, 1, CHANNELS)) > 0, 1.0, -1.0)
    scales = jnp.exp(jax.random.uniform(keys[3], (1, 1, 1, CHANNELS), jnp.float32, 0.0, 2.3))
    noise = jax.random.normal(keys[4], (BINS, 2, SEG, CHANNELS), jnp.float32)
    return ((0.8 * source * gains * signs + noise) * scales).astype(jnp.bfloat16)


def draw_valid(key, part):
    key = jax.random.fold_in(key, 23)
    keys = jax.random.split(key, 2)
    usable = (jax.random.randint(keys[0], (NB, SEG), 0, 4) < 3).astype(jnp.int32)
    dead_block = jax.random.randint(keys[1], (), 0, NB)
    block_ids = jnp.arange(NB, dtype=jnp.int32)[:, None]
    return jnp.where(block_ids == dead_block, 0, usable).astype(jnp.int32)


def setup_inputs(seed: int = 0) -> dict:
    arg_keys = jax.random.split(jax.random.key(seed), 3)
    return {
        "spectra": draw_spectra(jax.random.fold_in(arg_keys[2], 71), 0),
        "valid": draw_valid(jax.random.fold_in(arg_keys[2], 71), 0),
    }


def reference(spectra, valid):
    spectra32 = spectra.astype(jnp.float32)
    amplitude = lax.optimization_barrier(jnp.sum(jnp.sqrt(spectra32[:, 0] ** 2 + spectra32[:, 1] ** 2), axis=0))
    keep = jnp.repeat(valid.astype(jnp.float32).T, BLOCK, axis=1)
    white = (spectra32 / (amplitude / BINS + 1e-06) * keep).astype(jnp.bfloat16)
    maskf = valid.astype(jnp.float32)

    def one_row(index):
        left = lax.dynamic_slice_in_dim(white, index * BLOCK, BLOCK, 3).astype(jnp.float32)
        left_mask = lax.dynamic_slice_in_dim(maskf, index, 1, 0)[0]
        pieces = []
        for lag in range(NH):
            other = ((index + lag) % NB).astype(jnp.int32)
            right = lax.dynamic_slice_in_dim(white, other * BLOCK, BLOCK, 3).astype(jnp.float32)
            right_mask = lax.dynamic_slice_in_dim(maskf, other, 1, 0)[0]
            total = jnp.maximum(jnp.sum(left_mask * right_mask), 1.0)
            real_part = jnp.einsum('fsa,fsb->fab', left[:, 0], right[:, 0]) + jnp.einsum('fsa,fsb->fab', left[:, 1], right[:, 1])
            imag_part = jnp.einsum('fsa,fsb->fab', left[:, 1], right[:, 0]) - jnp.einsum('fsa,fsb->fab', left[:, 0], right[:, 1])
            pieces.append((jnp.stack([real_part, imag_part], axis=1) / total).astype(jnp.bfloat16))
        return jnp.stack(pieces)
    return lax.map(one_row, jnp.arange(NB, dtype=jnp.int32))
```

```python
import jax
import jax.numpy as jnp
from jax import lax
from jax.experimental import pallas as pl
from jax.experimental.pallas import tpu as pltpu
from jax.sharding import PartitionSpec as P

AXES = ("chan", "bin")
F32 = jnp.float32
BF16 = jnp.bfloat16
PLACES = [
    (p, z, y, x, c)
    for p in range(2)
    for z in range(4)
    for y in range(2)
    for x in range(4)
    for c in range(2)
]
MASK_ROWS = 16


def place(p, z, y, x, c):
    return (p * 4 + z) * 16 + (y * 4 + x) * 2 + c


def route(target):
    pairs = []
    for at in PLACES:
        to = target(*at)
        if to is not None:
            pairs.append((place(*at), place(*to)))
    return pairs


def chan_route(shift):
    def target(p, z, y, x, c):
        to = (p * 4 + z + shift) % 8
        return to // 4, to % 4, y, x, c

    return route(target)


DOWN = route(lambda p, z, y, x, c: (p, (z - 1) % 4, y, x, c))
UP = route(lambda p, z, y, x, c: (p, (z + 1) % 4, y, x, c))
CROSS = chan_route(4)
NEXT = chan_route(1)
CORE = route(lambda p, z, y, x, c: (p, z, y, x, 1 - c))
Y_LO = route(lambda p, z, y, x, c: (p, z, 1 - y, x, c))
X_BY = {d: route(lambda p, z, y, x, c, d=d: (p, z, y, (x + d) % 4, c)) for d in (1, 2, 3)}


def send(value, pairs):
    return lax.ppermute(value, AXES, pairs)


def tie(values):
    return lax.optimization_barrier(values)


def part_of(array, index, rows):
    return lax.dynamic_slice_in_dim(array, index * rows, rows, 0)


def sum_stage_a(partial, x, core):
    half = partial.shape[0] // 2
    mine = part_of(partial, core, half) + send(part_of(partial, 1 - core, half), CORE)
    quarter = half // 4
    own = part_of(mine, x, quarter)
    for d in (1, 2, 3):
        own = own + send(part_of(mine, (x + d) % 4, quarter), X_BY[d])
    return own


def sum_stage_b(own, x, core):
    quarter = own.shape[0]
    own = own + send(own, Y_LO)
    behind = [own] + [send(own, X_BY[d]) for d in (1, 2, 3)]
    line = jnp.concatenate(behind[::-1] * 2, axis=0)
    half = lax.dynamic_slice_in_dim(line, (3 - x) * quarter, 4 * quarter, 0)
    other = send(half, CORE)
    return jnp.where(
        core == 0,
        jnp.concatenate([half, other], axis=0),
        jnp.concatenate([other, half], axis=0),
    )


def pair_kernel(inv, x, y, d, u, sx, sy, sd, su, *rest):
    out, res, wx, wy, wd, wu, lx, ld = rest[-8:]
    width = 128
    depth = x.shape[2]

    def whiten(src, scale, dst):
        factor = scale[...].astype(F32)
        for part in range(2):
            dst[part * depth : (part + 1) * depth, :] = (
                src[0, part].astype(F32) * factor
            ).astype(BF16)

    def turn(src, dst):
        re = src[:depth, :].T
        im = src[depth:, :].T
        cols = re.shape[0]
        dst[:cols, :depth] = re
        dst[:cols, depth:] = im
        dst[cols:, :depth] = im
        dst[cols:, depth:] = -re

    whiten(x, sx, wx)
    whiten(d, sd, wd)
    turn(wx, lx)
    turn(wd, ld)
    whiten(y, sy, wy)
    whiten(u, su, wu)

    def cross(left, right, offset, write):
        both = jnp.dot(left[...], right[...], preferred_element_type=F32)
        for row in range(2):
            for col in range(2):
                factor = inv[offset * 4 + row * 2 + col]
                for part in range(2):
                    top = (part * 2 + row) * width
                    tile = both[top : top + width, col * width : (col + 1) * width]
                    write(row, col, part, (tile * factor).astype(BF16))

    def own_writer(offset):
        def write(row, col, part, tile):
            lag = 2 * offset + col - row
            if 0 <= lag <= 8:
                out[row, lag, 0, part] = tile

        return write

    def res_write(row, col, part, tile):
        res[row, col, 0, part] = tile

    cross(ld, wu, 2, res_write)
    cross(lx, wx, 0, own_writer(0))
    cross(lx, wd, 1, own_writer(1))
    cross(lx, wu, 3, own_writer(3))
    cross(lx, wy, 4, own_writer(4))


def pairs_of(chunk, inv, spectra, y, d, u, sx, sy, sd, su, out):
    bins_here, _, segs, chans = spectra.shape
    count = y.shape[0]
    base = chunk * count
    blk = (1, 2, segs, chans)
    scale = pl.BlockSpec((segs, chans), lambda f: (0, 0))
    local = pl.BlockSpec(blk, lambda f: (f, 0, 0, 0))
    in_specs = [
        pl.BlockSpec(memory_space=pltpu.SMEM),
        pl.BlockSpec(blk, lambda f: (base + f, 0, 0, 0)),
        local,
        local,
        local,
        scale,
        scale,
        scale,
        scale,
    ]
    args = [inv, spectra, y, d, u, sx, sy, sd, su]
    aliases = {}
    if out is not None:
        in_specs.append(pl.BlockSpec(memory_space=pl.ANY))
        aliases = {len(args): 0}
        args.append(out)
    return pl.pallas_call(
        pair_kernel,
        grid=(count,),
        in_specs=in_specs,
        out_specs=[
            pl.BlockSpec((2, 9, 1, 2, 128, 128), lambda f: (0, 0, base + f, 0, 0, 0)),
            pl.BlockSpec((2, 2, 1, 2, 128, 128), lambda f: (0, 0, f, 0, 0, 0)),
        ],
        out_shape=[
            jax.ShapeDtypeStruct((2, 9, bins_here, 2, 128, 128), BF16),
            jax.ShapeDtypeStruct((2, 2, count, 2, 128, 128), BF16),
        ],
        scratch_shapes=[pltpu.VMEM((2 * segs, chans), BF16)] * 4
        + [pltpu.VMEM((2 * chans, 2 * segs), BF16)] * 2,
        input_output_aliases=aliases,
        cost_estimate=pl.CostEstimate(
            flops=count * 5 * 2 * 512 * 1024 * 256,
            bytes_accessed=count * 4 * 1024 * 1024,
            transcendentals=0,
        ),
        compiler_params=pltpu.CompilerParams(vmem_limit_bytes=40 * 1024 * 1024),
    )(*args)


def place_kernel(res, old, out):
    out[...] = res[...]


def placed(chunk, res, out):
    count = res.shape[2]
    blk = (1, 1, count, 2, 128, 128)
    return pl.pallas_call(
        place_kernel,
        grid=(2, 2),
        in_specs=[
            pl.BlockSpec(blk, lambda row, col: (row, col, 0, 0, 0, 0)),
            pl.BlockSpec(memory_space=pl.ANY),
        ],
        out_specs=pl.BlockSpec(
            blk, lambda row, col: (row, 4 + col - row, chunk, 0, 0, 0)
        ),
        out_shape=jax.ShapeDtypeStruct(out.shape, out.dtype),
        input_output_aliases={1: 0},
        cost_estimate=pl.CostEstimate(
            flops=0, bytes_accessed=count * 512 * 1024, transcendentals=0
        ),
    )(res, out)


def shards(spectra, valid):
    bins_here = spectra.shape[0]
    segs, chans = spectra.shape[2:]
    bins = bins_here * lax.axis_size("bin")
    z = lax.axis_index("chan") % 4
    at = lax.axis_index("bin")
    core, x = at % 2, (at // 2) % 4
    chunks = 4
    count = bins_here // chunks
    own = [spectra[i * count : (i + 1) * count] for i in range(chunks)]
    Y, D, U, R = {}, {}, {}, {}
    mask = valid.astype(F32)

    def down_up(i):
        D[i] = send(jnp.where(z == 0, Y[i], own[i]), DOWN)
        U[i] = send(jnp.where(z == 3, own[i], Y[i]), UP)

    Y[0] = send(own[0], CROSS)
    wide = spectra.astype(F32)
    partial = jnp.sum(jnp.sqrt(wide[:, 0] ** 2 + wide[:, 1] ** 2), axis=0)
    piece = sum_stage_a(partial, x, core)
    Y[0], own[1], piece = tie((Y[0], own[1], piece))

    Y[1] = send(own[1], CROSS)
    down_up(0)
    amplitude = sum_stage_b(piece, x, core)
    keep = jnp.repeat(mask.T, chans // valid.shape[0], axis=1)
    sx = keep / (amplitude / bins + 1e-06)
    packed = jnp.concatenate(
        [
            sx.astype(BF16),
            valid.astype(BF16).reshape(-1, chans),
            jnp.zeros((MASK_ROWS - valid.size // chans, chans), BF16),
        ],
        axis=0,
    )
    Y[1], D[0], U[0], own[2], packed = tie((Y[1], D[0], U[0], own[2], packed))

    Y[2] = send(own[2], CROSS)
    down_up(1)
    S = {o: send(packed, chan_route(-o)) for o in (1, 3, 4)}
    Y[2], D[1], U[1], own[3], S = tie((Y[2], D[1], U[1], own[3], S))

    masks = {0: mask}
    for o in S:
        rows = S[o][segs : segs + valid.size // chans]
        masks[o] = rows.reshape(valid.shape).astype(F32)
    sides = [(0, 0), (0, 1), (1, 3), (0, 3), (0, 4)]
    left = jnp.stack([masks[a] for a, _ in sides])
    right = jnp.stack([masks[b] for _, b in sides])
    total = jnp.sum(left[:, :, None] * right[:, None], axis=-1)
    inv = (1.0 / jnp.maximum(total, 1.0)).reshape(-1)

    out = None

    def pairs(i):
        nonlocal out
        out, res = pairs_of(i, inv, spectra, Y[i], D[i], U[i], sx, S[4], S[1], S[3], out)
        R[i] = send(res, NEXT)

    Y[3] = send(own[3], CROSS)
    down_up(2)
    pairs(0)
    pairs(1)
    Y[3], D[2], U[2], R[0], R[1], out = tie((Y[3], D[2], U[2], R[0], R[1], out))

    down_up(3)
    pairs(2)
    for i in (0, 1):
        out = placed(i, R[i], out)
    D[3], U[3], R[2], out = tie((D[3], U[3], R[2], out))

    pairs(3)
    for i in (2, 3):
        out = placed(i, R[i], out)
    return out


def solution(mesh):
    return jax.shard_map(
        shards,
        mesh=mesh,
        in_specs=(P("bin", None, None, "chan"), P("chan", None)),
        out_specs=P("chan", None, "bin", None, None, None),
        check_vma=False,
    )
```

```python
import functools

import jax
import jax.numpy as jnp
from jax import lax
from jax.experimental import pallas as pl
from jax.experimental.pallas import tpu as pltpu
from jax.sharding import PartitionSpec as P

AXES = ("chan", "bin")
F32 = jnp.float32
BF16 = jnp.bfloat16
PLACES = [
    (p, z, y, x, c)
    for p in range(2)
    for z in range(4)
    for y in range(2)
    for x in range(4)
    for c in range(2)
]
VMEM = 40 * 1024 * 1024


def place(p, z, y, x, c):
    return (p * 4 + z) * 16 + (y * 4 + x) * 2 + c


def route(target):
    pairs = []
    for at in PLACES:
        to = target(*at)
        if to is not None:
            pairs.append((place(*at), place(*to)))
    return pairs


def chan_route(shift):
    def target(p, z, y, x, c):
        to = (p * 4 + z + shift) % 8
        return to // 4, to % 4, y, x, c

    return route(target)


DOWN = route(lambda p, z, y, x, c: (p, (z - 1) % 4, y, x, c))
UP = route(lambda p, z, y, x, c: (p, (z + 1) % 4, y, x, c))
CROSS = chan_route(4)
NEXT = chan_route(1)
CORE = route(lambda p, z, y, x, c: (p, z, y, x, 1 - c))
Y_LO = route(lambda p, z, y, x, c: (p, z, 1 - y, x, c))
X_BY = {d: route(lambda p, z, y, x, c, d=d: (p, z, y, (x + d) % 4, c)) for d in (1, 2, 3)}


def send(value, pairs):
    return lax.ppermute(value, AXES, pairs)


def tie(values):
    return lax.optimization_barrier(values)


def part_of(array, index, rows):
    return lax.dynamic_slice_in_dim(array, index * rows, rows, 0)


def sum_pieces(partial, x, core):
    half = partial.shape[0] // 2
    mine = part_of(partial, core, half) + send(part_of(partial, 1 - core, half), CORE)
    quarter = half // 4
    own = part_of(mine, x, quarter)
    for d in (1, 2, 3):
        own = own + send(part_of(mine, (x + d) % 4, quarter), X_BY[d])
    return own


def gather_x(own, x):
    quarter = own.shape[1]
    behind = [own] + [send(own, X_BY[d]) for d in (1, 2, 3)]
    line = jnp.concatenate(behind[::-1] * 2, axis=1)
    return lax.dynamic_slice_in_dim(line, (3 - x) * quarter, 4 * quarter, 1)


def gather_core(half, core):
    other = send(half, CORE)
    return jnp.where(
        core == 0,
        jnp.concatenate([half, other], axis=1),
        jnp.concatenate([other, half], axis=1),
    )


def whiten(src, factor, dst):
    depth = src.shape[1]
    factor = factor.astype(F32)
    for part in range(2):
        dst[part * depth : (part + 1) * depth, :] = (
            src[part].astype(F32) * factor
        ).astype(BF16)


def turn(src, dst):
    depth, cols = src.shape[0] // 2, src.shape[1]
    re = src[:depth, :].T
    im = src[depth:, :].T
    dst[:cols, :depth] = re
    dst[:cols, depth:] = im
    dst[cols:, :depth] = im
    dst[cols:, depth:] = -re


def cross(left, right, inv, side, write):
    both = jnp.dot(left[...], right[...], preferred_element_type=F32)
    width = both.shape[1] // 2
    for row in range(2):
        for col in range(2):
            factor = inv[side * 4 + row * 2 + col]
            for part in range(2):
                top = (part * 2 + row) * width
                tile = both[top : top + width, col * width : (col + 1) * width]
                write(row, col, part, (tile * factor).astype(BF16))


def pair_kernel(offsets, side, inv, scales, *rest):
    n = len(offsets)
    sources = rest[:n]
    out, res = rest[-n - 4 : -n - 2]
    white = rest[-n - 2 : -2]
    lx, ld = rest[-2:]

    for o, src, dst in zip(offsets, sources, white):
        whiten(src.at[0], scales[(0, 1, None, 2, 3)[o]], dst)
    turn(white[0], lx)
    turn(white[1], ld)

    def res_write(row, col, part, tile):
        res[row, col, 0, part] = tile

    cross(ld, white[-1], inv, side, res_write)
    for o, right in zip(offsets, white):

        def out_write(row, col, part, tile, o=o):
            lag = 2 * o + col - row
            if 0 <= lag <= 8:
                out[row, lag, 0, part] = tile

        cross(lx, right, inv, o, out_write)


def pairs_of(base, offsets, side, inv, scales, spectra, others, out):
    bins_here, _, segs, chans = spectra.shape
    count = others[0].shape[0]
    blk = (1, 2, segs, chans)
    in_specs = [
        pl.BlockSpec(memory_space=pltpu.SMEM),
        pl.BlockSpec(scales.shape, lambda f: (0, 0, 0)),
        pl.BlockSpec(blk, lambda f: (base + f, 0, 0, 0)),
    ] + [pl.BlockSpec(blk, lambda f: (f, 0, 0, 0))] * len(others)
    args = [inv, scales, spectra, *others]
    aliases = {}
    if out is not None:
        in_specs.append(pl.BlockSpec(memory_space=pl.ANY))
        aliases = {len(args): 0}
        args.append(out)
    return pl.pallas_call(
        functools.partial(pair_kernel, offsets, side),
        grid=(count,),
        in_specs=in_specs,
        out_specs=[
            pl.BlockSpec((2, 9, 1, 2, 128, 128), lambda f: (0, 0, base + f, 0, 0, 0)),
            pl.BlockSpec((2, 2, 1, 2, 128, 128), lambda f: (0, 0, f, 0, 0, 0)),
        ],
        out_shape=[
            jax.ShapeDtypeStruct((2, 9, bins_here, 2, 128, 128), BF16),
            jax.ShapeDtypeStruct((2, 2, count, 2, 128, 128), BF16),
        ],
        scratch_shapes=[pltpu.VMEM((2 * segs, chans), BF16)] * (len(others) + 1)
        + [pltpu.VMEM((2 * chans, 2 * segs), BF16)] * 2,
        input_output_aliases=aliases,
        cost_estimate=pl.CostEstimate(
            flops=count * 5 * 2 * 512 * 1024 * 256,
            bytes_accessed=count * 4 * 1024 * 1024,
            transcendentals=0,
        ),
        compiler_params=pltpu.CompilerParams(vmem_limit_bytes=VMEM),
    )(*args)


def place_kernel(res, old, out):
    out[...] = res[...]


def placed(base, offset, res, out):
    count = res.shape[2]
    blk = (1, 1, count, 2, 128, 128)
    return pl.pallas_call(
        place_kernel,
        grid=(2, 2),
        in_specs=[
            pl.BlockSpec(blk, lambda row, col: (row, col, 0, 0, 0, 0)),
            pl.BlockSpec(memory_space=pl.ANY),
        ],
        out_specs=pl.BlockSpec(
            blk, lambda row, col: (row, 2 * offset + col - row, base // count, 0, 0, 0)
        ),
        out_shape=jax.ShapeDtypeStruct(out.shape, out.dtype),
        input_output_aliases={1: 0},
        cost_estimate=pl.CostEstimate(
            flops=0, bytes_accessed=count * 512 * 1024, transcendentals=0
        ),
        compiler_params=pltpu.CompilerParams(vmem_limit_bytes=VMEM),
    )(res, out)


def last_kernel(base, spots, count, inv, scales, x, far, *rest):
    n = len(spots)
    incoming = rest[:n]
    out = rest[n + 1]
    wx, wf, lx, own = rest[n + 2 : n + 6]
    held = rest[n + 6 : 2 * n + 6]
    load_sems, store_sems = rest[2 * n + 6 :]
    step = pl.program_id(0)
    loads = [
        pltpu.make_async_copy(src, dst, load_sems.at[i])
        for i, (src, dst) in enumerate(zip(incoming, held))
    ]

    @pl.when(step == 0)
    def _():
        for copy in loads:
            copy.start()

    whiten(x.at[0], scales[0], wx)
    whiten(far.at[0], scales[1], wf)
    turn(wx, lx)

    def write(row, col, part, tile):
        own[row, col, step, part] = tile

    cross(lx, wf, inv, 2, write)

    @pl.when(step == count - 1)
    def _():
        stores = []
        for copy in loads:
            copy.wait()
        for i, (start, offset, src) in enumerate(
            [(base, 2, own)] + [(*spot, src) for spot, src in zip(spots, held)]
        ):
            for row in range(2):
                for col in range(2):
                    stores.append(
                        pltpu.make_async_copy(
                            src.at[row, col],
                            out.at[row, 2 * offset + col - row, pl.ds(start, count)],
                            store_sems.at[i * 4 + row * 2 + col],
                        )
                    )
        for copy in stores:
            copy.start()
        for copy in stores:
            copy.wait()


def last_of(base, inv, scales, spectra, far, spots, incoming, out):
    segs, chans = spectra.shape[2:]
    count = far.shape[0]
    n = len(spots)
    blk = (1, 2, segs, chans)
    anywhere = pl.BlockSpec(memory_space=pl.ANY)
    res_shape = incoming[0].shape
    return pl.pallas_call(
        functools.partial(last_kernel, base, spots, count),
        grid=(count,),
        in_specs=[
            pl.BlockSpec(memory_space=pltpu.SMEM),
            pl.BlockSpec(scales.shape, lambda f: (0, 0, 0)),
            pl.BlockSpec(blk, lambda f: (base + f, 0, 0, 0)),
            pl.BlockSpec(blk, lambda f: (f, 0, 0, 0)),
        ]
        + [anywhere] * (n + 1),
        out_specs=anywhere,
        out_shape=jax.ShapeDtypeStruct(out.shape, out.dtype),
        scratch_shapes=[pltpu.VMEM((2 * segs, chans), BF16)] * 2
        + [pltpu.VMEM((2 * chans, 2 * segs), BF16)]
        + [pltpu.VMEM(res_shape, BF16)] * (n + 1)
        + [pltpu.SemaphoreType.DMA((n,)), pltpu.SemaphoreType.DMA((4 * (n + 1),))],
        input_output_aliases={4 + n: 0},
        cost_estimate=pl.CostEstimate(
            flops=count * 2 * 512 * 1024 * 256,
            bytes_accessed=count * 4 * 1024 * 1024,
            transcendentals=0,
        ),
        compiler_params=pltpu.CompilerParams(vmem_limit_bytes=VMEM),
    )(inv, scales, spectra, far, *incoming, out)


def shards(spectra, valid):
    bins_here = spectra.shape[0]
    segs, chans = spectra.shape[2:]
    bins = bins_here * lax.axis_size("bin")
    z = lax.axis_index("chan") % 4
    at = lax.axis_index("bin")
    core, x = at % 2, (at // 2) % 4
    chunks = 4
    count = bins_here // chunks
    own = [spectra[i * count : (i + 1) * count] for i in range(chunks)]
    Y, D, U, R = {}, {}, {}, {}

    def for_down(i):
        return jnp.where(z == 0, Y[i], own[i])

    def for_up(i):
        return jnp.where(z == 3, own[i], Y[i])

    own[0], spectra0, valid0 = tie((own[0], spectra, valid))
    Y[0] = send(own[0], CROSS)
    wide = spectra0.astype(F32)
    partial = jnp.sum(jnp.sqrt(wide[:, 0] ** 2 + wide[:, 1] ** 2), axis=0)
    piece = sum_pieces(partial, x, core)
    masks = {o: send(valid0, chan_route(-o)) for o in (1, 2, 3, 4)}
    masks[0] = valid0
    Y[0], own[1], piece, masks = tie((Y[0], own[1], piece, masks))

    below, above = for_down(0), for_up(0)
    below, above, piece, masks = tie((below, above, piece, masks))
    D[0], U[0] = send(below, DOWN), send(above, UP)
    Y[1] = send(own[1], CROSS)
    amplitude = piece + send(piece, Y_LO)
    rows = amplitude.shape[0]
    here = part_of(valid.astype(F32).T, core * 4 + x, rows)
    keep = jnp.repeat(here, chans // valid.shape[0], axis=1)
    scale = (keep / (amplitude / bins + 1e-06)).astype(BF16)
    sides = [(0, 0), (0, 1), (0, 2), (0, 3), (0, 4), (1, 3), (1, 4)]
    left = jnp.stack([masks[a] for a, _ in sides]).astype(F32)
    right = jnp.stack([masks[b] for _, b in sides]).astype(F32)
    total = jnp.sum(left[:, :, None] * right[:, None], axis=-1)
    inv = (1.0 / jnp.maximum(total, 1.0)).reshape(-1)
    Y[1], D[0], U[0], own[2], scale, inv = tie((Y[1], D[0], U[0], own[2], scale, inv))

    below, above = for_down(1), for_up(1)
    below, above, scale = tie((below, above, scale))
    D[1], U[1] = send(below, DOWN), send(above, UP)
    Y[2] = send(own[2], CROSS)
    far = [scale] + [send(scale, chan_route(-o)) for o in (1, 3, 4)]
    Y[2], D[1], U[1], own[3], far = tie((Y[2], D[1], U[1], own[3], far))

    below, above = for_down(2), for_up(2)
    below, above, far = tie((below, above, far))
    D[2], U[2] = send(below, DOWN), send(above, UP)
    Y[3] = send(own[3], CROSS)
    scales = gather_core(gather_x(jnp.stack(far), x), core)
    out = None
    res = {}

    def pairs(i, offsets, side, others):
        nonlocal out
        out, res[i] = pairs_of(
            i * count, offsets, side, inv, scales, spectra, others, out
        )

    Y[3], D[2], U[2], scales, inv = tie((Y[3], D[2], U[2], scales, inv))

    pairs(0, (0, 1, 4, 3), 5, (D[0], Y[0], U[0]))
    R[0] = send(res[0], NEXT)
    D[3] = send(for_down(3), DOWN)
    scale2 = send(scales[1], chan_route(-1))
    pairs(1, (0, 1, 4, 3), 5, (D[1], Y[1], U[1]))
    R[1] = send(res[1], NEXT)
    pairs(2, (0, 1, 4, 3), 5, (D[2], Y[2], U[2]))
    D[3], R[0], R[1], out, res[2], scale2 = tie(
        (D[3], R[0], R[1], out, res[2], scale2)
    )

    far2 = send(D[3], chan_route(-1))
    R[2] = send(res[2], NEXT)
    pairs(3, (0, 1, 4), 6, (D[3], Y[3]))
    R[3] = send(res[3], NEXT)
    for i in (0, 1):
        out = placed(i * count, 2, R[i], out)
    return last_of(
        3 * count,
        inv,
        jnp.stack([scales[0], scale2]),
        spectra,
        far2,
        ((2 * count, 2), (3 * count, 3)),
        (R[2], R[3]),
        out,
    )


def solution(mesh):
    return jax.shard_map(
        shards,
        mesh=mesh,
        in_specs=(P("bin", None, None, "chan"), P("chan", None)),
        out_specs=P("chan", None, "bin", None, None, None),
        check_vma=False,
    )
```

```python
import functools

import jax
import jax.numpy as jnp
from jax import lax
from jax.experimental import pallas as pl
from jax.experimental.pallas import tpu as pltpu
from jax.sharding import PartitionSpec as P

AXES = ("chan", "bin")
F32 = jnp.float32
BF16 = jnp.bfloat16
PLACES = [
    (p, z, y, x, c)
    for p in range(2)
    for z in range(4)
    for y in range(2)
    for x in range(4)
    for c in range(2)
]
VMEM = 40 * 1024 * 1024


def place(p, z, y, x, c):
    return (p * 4 + z) * 16 + (y * 4 + x) * 2 + c


def route(target):
    pairs = []
    for at in PLACES:
        to = target(*at)
        if to is not None:
            pairs.append((place(*at), place(*to)))
    return pairs


def chan_route(shift):
    def target(p, z, y, x, c):
        to = (p * 4 + z + shift) % 8
        return to // 4, to % 4, y, x, c

    return route(target)


DOWN = route(lambda p, z, y, x, c: (p, (z - 1) % 4, y, x, c))
UP = route(lambda p, z, y, x, c: (p, (z + 1) % 4, y, x, c))
CROSS = chan_route(4)
NEXT = chan_route(1)
CORE = route(lambda p, z, y, x, c: (p, z, y, x, 1 - c))
Y_LO = route(lambda p, z, y, x, c: (p, z, 1 - y, x, c))
X_BY = {d: route(lambda p, z, y, x, c, d=d: (p, z, y, (x + d) % 4, c)) for d in (1, 2, 3)}


def send(value, pairs):
    return lax.ppermute(value, AXES, pairs)


def tie(values):
    return lax.optimization_barrier(values)


def part_of(array, index, rows):
    return lax.dynamic_slice_in_dim(array, index * rows, rows, 0)


def sum_pieces(partial, x, core):
    half = partial.shape[0] // 2
    mine = part_of(partial, core, half) + send(part_of(partial, 1 - core, half), CORE)
    quarter = half // 4
    own = part_of(mine, x, quarter)
    for d in (1, 2, 3):
        own = own + send(part_of(mine, (x + d) % 4, quarter), X_BY[d])
    return own


def gather_x(own, x):
    quarter = own.shape[1]
    behind = [own] + [send(own, X_BY[d]) for d in (1, 2, 3)]
    line = jnp.concatenate(behind[::-1] * 2, axis=1)
    return lax.dynamic_slice_in_dim(line, (3 - x) * quarter, 4 * quarter, 1)


def gather_core(half, core):
    other = send(half, CORE)
    return jnp.where(
        core == 0,
        jnp.concatenate([half, other], axis=1),
        jnp.concatenate([other, half], axis=1),
    )


def whiten(src, factor, dst):
    depth = src.shape[1]
    factor = factor.astype(F32)
    for part in range(2):
        dst[part * depth : (part + 1) * depth, :] = (
            src[part].astype(F32) * factor
        ).astype(BF16)


def turn(src, dst):
    depth, cols = src.shape[0] // 2, src.shape[1]
    re = src[:depth, :].T
    im = src[depth:, :].T
    dst[:cols, :depth] = re
    dst[:cols, depth:] = im
    dst[cols:, :depth] = im
    dst[cols:, depth:] = -re


def cross(left, right, inv, side, write):
    both = jnp.dot(left[...], right[...], preferred_element_type=F32)
    width = both.shape[1] // 2
    for row in range(2):
        for col in range(2):
            factor = inv[side * 4 + row * 2 + col]
            for part in range(2):
                top = (part * 2 + row) * width
                tile = both[top : top + width, col * width : (col + 1) * width]
                write(row, col, part, (tile * factor).astype(BF16))


def pair_kernel(offsets, side, inv, scales, *rest):
    n = len(offsets)
    sources = rest[:n]
    out, res = rest[-n - 4 : -n - 2]
    white = rest[-n - 2 : -2]
    lx, ld = rest[-2:]

    for o, src, dst in zip(offsets, sources, white):
        whiten(src.at[0], scales[(0, 1, None, 2, 3)[o]], dst)
    turn(white[0], lx)
    turn(white[1], ld)

    def res_write(row, col, part, tile):
        res[row, col, 0, part] = tile

    cross(ld, white[-1], inv, side, res_write)
    for o, right in zip(offsets, white):

        def out_write(row, col, part, tile, o=o):
            lag = 2 * o + col - row
            if 0 <= lag <= 8:
                out[row, lag, 0, part] = tile

        cross(lx, right, inv, o, out_write)


def pairs_of(base, count, offsets, side, inv, scales, spectra, others, out):
    bins_here, _, segs, chans = spectra.shape
    blk = (1, 2, segs, chans)
    in_specs = [
        pl.BlockSpec(memory_space=pltpu.SMEM),
        pl.BlockSpec(scales.shape, lambda f: (0, 0, 0)),
        pl.BlockSpec(blk, lambda f: (base + f, 0, 0, 0)),
    ] + [pl.BlockSpec(blk, lambda f, at=at: (at + f, 0, 0, 0)) for _, at in others]
    args = [inv, scales, spectra] + [array for array, _ in others]
    aliases = {}
    if out is not None:
        in_specs.append(pl.BlockSpec(memory_space=pl.ANY))
        aliases = {len(args): 0}
        args.append(out)
    return pl.pallas_call(
        functools.partial(pair_kernel, offsets, side),
        grid=(count,),
        in_specs=in_specs,
        out_specs=[
            pl.BlockSpec((2, 9, 1, 2, 128, 128), lambda f: (0, 0, base + f, 0, 0, 0)),
            pl.BlockSpec((2, 2, 1, 2, 128, 128), lambda f: (0, 0, f, 0, 0, 0)),
        ],
        out_shape=[
            jax.ShapeDtypeStruct((2, 9, bins_here, 2, 128, 128), BF16),
            jax.ShapeDtypeStruct((2, 2, count, 2, 128, 128), BF16),
        ],
        scratch_shapes=[pltpu.VMEM((2 * segs, chans), BF16)] * (len(others) + 1)
        + [pltpu.VMEM((2 * chans, 2 * segs), BF16)] * 2,
        input_output_aliases=aliases,
        cost_estimate=pl.CostEstimate(
            flops=count * 5 * 2 * 512 * 1024 * 256,
            bytes_accessed=count * 4 * 1024 * 1024,
            transcendentals=0,
        ),
        compiler_params=pltpu.CompilerParams(vmem_limit_bytes=VMEM),
    )(*args)


def place_kernel(res, old, out):
    out[...] = res[...]


def placed(base, offset, res, out):
    count = res.shape[2]
    blk = (1, 1, count, 2, 128, 128)
    return pl.pallas_call(
        place_kernel,
        grid=(2, 2),
        in_specs=[
            pl.BlockSpec(blk, lambda row, col: (row, col, 0, 0, 0, 0)),
            pl.BlockSpec(memory_space=pl.ANY),
        ],
        out_specs=pl.BlockSpec(
            blk, lambda row, col: (row, 2 * offset + col - row, base // count, 0, 0, 0)
        ),
        out_shape=jax.ShapeDtypeStruct(out.shape, out.dtype),
        input_output_aliases={1: 0},
        cost_estimate=pl.CostEstimate(
            flops=0, bytes_accessed=count * 512 * 1024, transcendentals=0
        ),
        compiler_params=pltpu.CompilerParams(vmem_limit_bytes=VMEM),
    )(res, out)


def last_kernel(base, spots, count, inv, scales, x, far, *rest):
    n = len(spots)
    incoming = rest[:n]
    out = rest[n + 1]
    wx, wf, lx, own = rest[n + 2 : n + 6]
    held = rest[n + 6 : 2 * n + 6]
    load_sems, store_sems = rest[2 * n + 6 :]
    step = pl.program_id(0)
    loads = [
        pltpu.make_async_copy(src, dst, load_sems.at[i])
        for i, (src, dst) in enumerate(zip(incoming, held))
    ]

    @pl.when(step == 0)
    def _():
        for copy in loads:
            copy.start()

    whiten(x.at[0], scales[0], wx)
    depth = far.shape[2]
    wf[:depth, :] = far[0, 0]
    wf[depth:, :] = far[0, 1]
    turn(wx, lx)

    def write(row, col, part, tile):
        own[row, col, step, part] = tile

    cross(lx, wf, inv, 2, write)

    @pl.when(step == count - 1)
    def _():
        stores = []
        for copy in loads:
            copy.wait()
        for i, (start, offset, src) in enumerate(
            [(base, 2, own)] + [(*spot, src) for spot, src in zip(spots, held)]
        ):
            for row in range(2):
                for col in range(2):
                    stores.append(
                        pltpu.make_async_copy(
                            src.at[row, col],
                            out.at[
                                row, 2 * offset + col - row, pl.ds(start, src.shape[2])
                            ],
                            store_sems.at[i * 4 + row * 2 + col],
                        )
                    )
        for copy in stores:
            copy.start()
        for copy in stores:
            copy.wait()


def last_of(base, inv, scales, spectra, far, spots, incoming, out):
    segs, chans = spectra.shape[2:]
    count = far.shape[0]
    n = len(spots)
    blk = (1, 2, segs, chans)
    anywhere = pl.BlockSpec(memory_space=pl.ANY)
    return pl.pallas_call(
        functools.partial(last_kernel, base, spots, count),
        grid=(count,),
        in_specs=[
            pl.BlockSpec(memory_space=pltpu.SMEM),
            pl.BlockSpec(scales.shape, lambda f: (0, 0, 0)),
            pl.BlockSpec(blk, lambda f: (base + f, 0, 0, 0)),
            pl.BlockSpec(blk, lambda f: (f, 0, 0, 0)),
        ]
        + [anywhere] * (n + 1),
        out_specs=anywhere,
        out_shape=jax.ShapeDtypeStruct(out.shape, out.dtype),
        scratch_shapes=[pltpu.VMEM((2 * segs, chans), BF16)] * 2
        + [pltpu.VMEM((2 * chans, 2 * segs), BF16)]
        + [pltpu.VMEM((2, 2, count, 2, 128, 128), BF16)]
        + [pltpu.VMEM(res.shape, BF16) for res in incoming]
        + [pltpu.SemaphoreType.DMA((n,)), pltpu.SemaphoreType.DMA((4 * (n + 1),))],
        input_output_aliases={4 + n: 0},
        cost_estimate=pl.CostEstimate(
            flops=count * 2 * 512 * 1024 * 256,
            bytes_accessed=count * 4 * 1024 * 1024,
            transcendentals=0,
        ),
        compiler_params=pltpu.CompilerParams(vmem_limit_bytes=VMEM),
    )(inv, scales, spectra, far, *incoming, out)


def shards(spectra, valid):
    bins_here = spectra.shape[0]
    segs, chans = spectra.shape[2:]
    bins = bins_here * lax.axis_size("bin")
    z = lax.axis_index("chan") % 4
    at = lax.axis_index("bin")
    core, x = at % 2, (at // 2) % 4
    chunks = 4
    count = bins_here // chunks
    own = [spectra[i * count : (i + 1) * count] for i in range(chunks)]
    Y, D, U, R, res = {}, {}, {}, {}, {}

    def for_down(i):
        return jnp.where(z == 0, Y[i], own[i])

    def for_up(i):
        return jnp.where(z == 3, own[i], Y[i])

    own[0], spectra0, valid0 = tie((own[0], spectra, valid))
    Y[0] = send(own[0], CROSS)
    wide = spectra0.astype(F32)
    partial = jnp.sum(jnp.sqrt(wide[:, 0] ** 2 + wide[:, 1] ** 2), axis=0)
    piece = sum_pieces(partial, x, core)
    masks = {o: send(valid0, chan_route(-o)) for o in (1, 2, 3, 4)}
    masks[0] = valid0
    Y[0], piece, masks = tie((Y[0], piece, masks))

    below, above = for_down(0), for_up(0)
    below, above, masks, piece = tie((below, above, masks, piece))
    D[0], U[0] = send(below, DOWN), send(above, UP)
    Y[1] = send(own[1], CROSS)
    amplitude = piece + send(piece, Y_LO)
    rows = amplitude.shape[0]
    here = part_of(valid.astype(F32).T, core * 4 + x, rows)
    keep = jnp.repeat(here, chans // valid.shape[0], axis=1)
    scale = (keep / (amplitude / bins + 1e-06)).astype(BF16)
    sides = [(0, 0), (0, 1), (0, 2), (0, 3), (0, 4), (1, 3), (1, 4)]
    left = jnp.stack([masks[a] for a, _ in sides]).astype(F32)
    right = jnp.stack([masks[b] for _, b in sides]).astype(F32)
    total = jnp.sum(left[:, :, None] * right[:, None], axis=-1)
    inv = (1.0 / jnp.maximum(total, 1.0)).reshape(-1)
    Y[1], D[0], U[0] = tie((Y[1], D[0], U[0]))
    Y[1], own[2], inv, scale = tie((Y[1], own[2], inv, scale))

    below, above = for_down(1), for_up(1)
    below, above, scale, D[0], U[0] = tie((below, above, scale, D[0], U[0]))
    D[1], U[1] = send(below, DOWN), send(above, UP)
    Y[2] = send(own[2], CROSS)
    far = [scale] + [send(scale, chan_route(-o)) for o in (1, 3, 4)]
    Y[2], D[1], U[1] = tie((Y[2], D[1], U[1]))
    Y[2], own[3], far = tie((Y[2], own[3], far))

    below, above = for_down(2), for_up(2)
    below, above, far, D[1], U[1] = tie((below, above, far, D[1], U[1]))
    D[2], U[2] = send(below, DOWN), send(above, UP)
    Y[3] = send(own[3], CROSS)
    scales = gather_core(gather_x(jnp.stack(far), x), core)
    out = None

    def pairs(i, base, n, offsets, side, others):
        nonlocal out
        out, res[i] = pairs_of(
            base, n, offsets, side, inv, scales, spectra, others, out
        )

    def whole(i):
        three = ((D[i], 0), (Y[i], 0), (U[i], 0))
        pairs(i, i * count, count, (0, 1, 4, 3), 5, three)

    whole(0)
    R[0] = send(res[0], NEXT)
    Y[3], D[2], U[2] = tie((Y[3], D[2], U[2]))
    Y[3], scales, out = tie((Y[3], scales, out))

    def whitened(block):
        return (block.astype(F32) * scales[1].astype(F32)).astype(BF16)

    below = for_down(3)
    below, D[2], U[2], scales = tie((below, D[2], U[2], scales))
    half = count // 2
    last = 3 * count
    first, second = send(below[:half], DOWN), send(below[half:], DOWN)
    whole(1)
    R[1] = send(res[1], NEXT)
    whole(2)
    R[2] = send(res[2], NEXT)
    first, R[0], out = tie((first, R[0], out))

    beyond = send(whitened(first), chan_route(-1))
    pairs(3, last, half, (0, 1, 4), 6, ((first, 0), (Y[3], 0)))
    R[3] = send(res[3], NEXT)
    second, R[1], out = tie((second, R[1], out))
    beyond2 = send(whitened(second), chan_route(-1))
    pairs(4, last + half, half, (0, 1, 4), 6, ((second, 0), (Y[3], half)))
    R[4] = send(res[4], NEXT)
    for i in (0, 1):
        out = placed(i * count, 2, R[i], out)
    out = last_of(last, inv, scales, spectra, beyond, ((2 * count, 2),), (R[2],), out)
    return last_of(
        last + half,
        inv,
        scales,
        spectra,
        beyond2,
        ((last, 3), (last + half, 3)),
        (R[3], R[4]),
        out,
    )


def solution(mesh):
    return jax.shard_map(
        shards,
        mesh=mesh,
        in_specs=(P("bin", None, None, "chan"), P("chan", None)),
        out_specs=P("chan", None, "bin", None, None, None),
        check_vma=False,
    )
```

```python
import functools

import jax
import jax.numpy as jnp
from jax import lax
from jax.experimental import pallas as pl
from jax.experimental.pallas import tpu as pltpu
from jax.sharding import PartitionSpec as P

AXES = ("chan", "bin")
F32 = jnp.float32
BF16 = jnp.bfloat16
PLACES = [
    (p, z, y, x, c)
    for p in range(2)
    for z in range(4)
    for y in range(2)
    for x in range(4)
    for c in range(2)
]
VMEM = 40 * 1024 * 1024


def place(p, z, y, x, c):
    return (p * 4 + z) * 16 + (y * 4 + x) * 2 + c


def route(target):
    pairs = []
    for at in PLACES:
        to = target(*at)
        if to is not None:
            pairs.append((place(*at), place(*to)))
    return pairs


def chan_route(shift):
    def target(p, z, y, x, c):
        to = (p * 4 + z + shift) % 8
        return to // 4, to % 4, y, x, c

    return route(target)


DOWN = route(lambda p, z, y, x, c: (p, (z - 1) % 4, y, x, c))
UP = route(lambda p, z, y, x, c: (p, (z + 1) % 4, y, x, c))
CROSS = chan_route(4)
NEXT = chan_route(1)
CORE = route(lambda p, z, y, x, c: (p, z, y, x, 1 - c))
Y_LO = route(lambda p, z, y, x, c: (p, z, 1 - y, x, c))
X_BY = {d: route(lambda p, z, y, x, c, d=d: (p, z, y, (x + d) % 4, c)) for d in (1, 2, 3)}


def send(value, pairs):
    return lax.ppermute(value, AXES, pairs)


def tie(values):
    return lax.optimization_barrier(values)


def part_of(array, index, rows):
    return lax.dynamic_slice_in_dim(array, index * rows, rows, 0)


def sum_pieces(partial, x, core):
    half = partial.shape[0] // 2
    mine = part_of(partial, core, half) + send(part_of(partial, 1 - core, half), CORE)
    quarter = half // 4
    own = part_of(mine, x, quarter)
    for d in (1, 2, 3):
        own = own + send(part_of(mine, (x + d) % 4, quarter), X_BY[d])
    return own


def gather_x(own, x):
    quarter = own.shape[1]
    behind = [own] + [send(own, X_BY[d]) for d in (1, 2, 3)]
    line = jnp.concatenate(behind[::-1] * 2, axis=1)
    return lax.dynamic_slice_in_dim(line, (3 - x) * quarter, 4 * quarter, 1)


def gather_core(half, core):
    other = send(half, CORE)
    return jnp.where(
        core == 0,
        jnp.concatenate([half, other], axis=1),
        jnp.concatenate([other, half], axis=1),
    )


def whiten(src, factor, dst):
    depth = src.shape[1]
    factor = factor.astype(F32)
    for part in range(2):
        dst[part * depth : (part + 1) * depth, :] = (
            src[part].astype(F32) * factor
        ).astype(BF16)


def turn(src, dst):
    depth, cols = src.shape[0] // 2, src.shape[1]
    re = src[:depth, :].T
    im = src[depth:, :].T
    dst[:cols, :depth] = re
    dst[:cols, depth:] = im
    dst[cols:, :depth] = im
    dst[cols:, depth:] = -re


def cross(left, right, inv, side, write):
    both = jnp.dot(left[...], right[...], preferred_element_type=F32)
    width = both.shape[1] // 2
    for row in range(2):
        for col in range(2):
            factor = inv[side * 4 + row * 2 + col]
            for part in range(2):
                top = (part * 2 + row) * width
                tile = both[top : top + width, col * width : (col + 1) * width]
                write(row, col, part, (tile * factor).astype(BF16))


def pair_kernel(offsets, side, inv, scales, *rest):
    n = len(offsets)
    sources = rest[:n]
    out, res = rest[-n - 4 : -n - 2]
    white = rest[-n - 2 : -2]
    lx, ld = rest[-2:]

    for o, src, dst in zip(offsets, sources, white):
        whiten(src.at[0], scales[(0, 1, None, 2, 3)[o]], dst)
    turn(white[0], lx)
    turn(white[1], ld)

    def res_write(row, col, part, tile):
        res[row, col, 0, part] = tile

    cross(ld, white[-1], inv, side, res_write)
    for o, right in zip(offsets, white):

        def out_write(row, col, part, tile, o=o):
            lag = 2 * o + col - row
            if 0 <= lag <= 8:
                out[row, lag, 0, part] = tile

        cross(lx, right, inv, o, out_write)


def pairs_of(base, count, offsets, side, inv, scales, spectra, others, out):
    bins_here, _, segs, chans = spectra.shape
    blk = (1, 2, segs, chans)
    in_specs = [
        pl.BlockSpec(memory_space=pltpu.SMEM),
        pl.BlockSpec(scales.shape, lambda f: (0, 0, 0)),
        pl.BlockSpec(blk, lambda f: (base + f, 0, 0, 0)),
    ] + [pl.BlockSpec(blk, lambda f, at=at: (at + f, 0, 0, 0)) for _, at in others]
    args = [inv, scales, spectra] + [array for array, _ in others]
    aliases = {}
    if out is not None:
        in_specs.append(pl.BlockSpec(memory_space=pl.ANY))
        aliases = {len(args): 0}
        args.append(out)
    return pl.pallas_call(
        functools.partial(pair_kernel, offsets, side),
        grid=(count,),
        in_specs=in_specs,
        out_specs=[
            pl.BlockSpec((2, 9, 1, 2, 128, 128), lambda f: (0, 0, base + f, 0, 0, 0)),
            pl.BlockSpec((2, 2, 1, 2, 128, 128), lambda f: (0, 0, f, 0, 0, 0)),
        ],
        out_shape=[
            jax.ShapeDtypeStruct((2, 9, bins_here, 2, 128, 128), BF16),
            jax.ShapeDtypeStruct((2, 2, count, 2, 128, 128), BF16),
        ],
        scratch_shapes=[pltpu.VMEM((2 * segs, chans), BF16)] * (len(others) + 1)
        + [pltpu.VMEM((2 * chans, 2 * segs), BF16)] * 2,
        input_output_aliases=aliases,
        cost_estimate=pl.CostEstimate(
            flops=count * 5 * 2 * 512 * 1024 * 256,
            bytes_accessed=count * 4 * 1024 * 1024,
            transcendentals=0,
        ),
        compiler_params=pltpu.CompilerParams(vmem_limit_bytes=VMEM),
    )(*args)


def place_kernel(res, old, out):
    out[...] = res[...]


def placed(base, offset, res, out):
    count = res.shape[2]
    blk = (1, 1, count, 2, 128, 128)
    return pl.pallas_call(
        place_kernel,
        grid=(2, 2),
        in_specs=[
            pl.BlockSpec(blk, lambda row, col: (row, col, 0, 0, 0, 0)),
            pl.BlockSpec(memory_space=pl.ANY),
        ],
        out_specs=pl.BlockSpec(
            blk, lambda row, col: (row, 2 * offset + col - row, base // count, 0, 0, 0)
        ),
        out_shape=jax.ShapeDtypeStruct(out.shape, out.dtype),
        input_output_aliases={1: 0},
        cost_estimate=pl.CostEstimate(
            flops=0, bytes_accessed=count * 512 * 1024, transcendentals=0
        ),
        compiler_params=pltpu.CompilerParams(vmem_limit_bytes=VMEM),
    )(res, out)


def last_kernel(base, spots, count, inv, scales, x, far, *rest):
    n = len(spots)
    incoming = rest[:n]
    out = rest[n + 1]
    wx, wf, lx, own = rest[n + 2 : n + 6]
    held = rest[n + 6 : 2 * n + 6]
    load_sems, store_sems = rest[2 * n + 6 :]
    step = pl.program_id(0)
    loads = [
        pltpu.make_async_copy(src, dst, load_sems.at[i])
        for i, (src, dst) in enumerate(zip(incoming, held))
    ]

    @pl.when(step == 0)
    def _():
        for copy in loads:
            copy.start()

    whiten(x.at[0], scales[0], wx)
    depth = far.shape[2]
    wf[:depth, :] = far[0, 0]
    wf[depth:, :] = far[0, 1]
    turn(wx, lx)

    def write(row, col, part, tile):
        own[row, col, step, part] = tile

    cross(lx, wf, inv, 2, write)

    @pl.when(step == count - 1)
    def _():
        stores = []
        for copy in loads:
            copy.wait()
        for i, (start, offset, src) in enumerate(
            [(base, 2, own)] + [(*spot, src) for spot, src in zip(spots, held)]
        ):
            for row in range(2):
                for col in range(2):
                    stores.append(
                        pltpu.make_async_copy(
                            src.at[row, col],
                            out.at[
                                row, 2 * offset + col - row, pl.ds(start, src.shape[2])
                            ],
                            store_sems.at[i * 4 + row * 2 + col],
                        )
                    )
        for copy in stores:
            copy.start()
        for copy in stores:
            copy.wait()


def last_of(base, inv, scales, spectra, far, spots, incoming, out):
    segs, chans = spectra.shape[2:]
    count = far.shape[0]
    n = len(spots)
    blk = (1, 2, segs, chans)
    anywhere = pl.BlockSpec(memory_space=pl.ANY)
    return pl.pallas_call(
        functools.partial(last_kernel, base, spots, count),
        grid=(count,),
        in_specs=[
            pl.BlockSpec(memory_space=pltpu.SMEM),
            pl.BlockSpec(scales.shape, lambda f: (0, 0, 0)),
            pl.BlockSpec(blk, lambda f: (base + f, 0, 0, 0)),
            pl.BlockSpec(blk, lambda f: (f, 0, 0, 0)),
        ]
        + [anywhere] * (n + 1),
        out_specs=anywhere,
        out_shape=jax.ShapeDtypeStruct(out.shape, out.dtype),
        scratch_shapes=[pltpu.VMEM((2 * segs, chans), BF16)] * 2
        + [pltpu.VMEM((2 * chans, 2 * segs), BF16)]
        + [pltpu.VMEM((2, 2, count, 2, 128, 128), BF16)]
        + [pltpu.VMEM(res.shape, BF16) for res in incoming]
        + [pltpu.SemaphoreType.DMA((n,)), pltpu.SemaphoreType.DMA((4 * (n + 1),))],
        input_output_aliases={4 + n: 0},
        cost_estimate=pl.CostEstimate(
            flops=count * 2 * 512 * 1024 * 256,
            bytes_accessed=count * 4 * 1024 * 1024,
            transcendentals=0,
        ),
        compiler_params=pltpu.CompilerParams(vmem_limit_bytes=VMEM),
    )(inv, scales, spectra, far, *incoming, out)


def shards(spectra, valid):
    bins_here = spectra.shape[0]
    segs, chans = spectra.shape[2:]
    bins = bins_here * lax.axis_size("bin")
    z = lax.axis_index("chan") % 4
    at = lax.axis_index("bin")
    core, x = at % 2, (at // 2) % 4
    chunks = 4
    count = bins_here // chunks
    own = [spectra[i * count : (i + 1) * count] for i in range(chunks)]
    Y, D, U, R, res = {}, {}, {}, {}, {}

    def for_down(i):
        return jnp.where(z == 0, Y[i], own[i])

    def for_up(i):
        return jnp.where(z == 3, own[i], Y[i])

    own[0], spectra0, valid0 = tie((own[0], spectra, valid))
    Y[0] = send(own[0], CROSS)
    wide = spectra0.astype(F32)
    partial = jnp.sum(jnp.sqrt(wide[:, 0] ** 2 + wide[:, 1] ** 2), axis=0)
    piece = sum_pieces(partial, x, core)
    masks = {o: send(valid0, chan_route(-o)) for o in (1, 2, 3, 4)}
    masks[0] = valid0
    Y[0], piece, masks = tie((Y[0], piece, masks))

    below, above = for_down(0), for_up(0)
    below, above, masks, piece = tie((below, above, masks, piece))
    D[0], U[0] = send(below, DOWN), send(above, UP)
    Y[1] = send(own[1], CROSS)
    amplitude = piece + send(piece, Y_LO)
    rows = amplitude.shape[0]
    here = part_of(valid.astype(F32).T, core * 4 + x, rows)
    keep = jnp.repeat(here, chans // valid.shape[0], axis=1)
    scale = (keep / (amplitude / bins + 1e-06)).astype(BF16)
    sides = [(0, 0), (0, 1), (0, 2), (0, 3), (0, 4), (1, 3), (1, 4)]
    left = jnp.stack([masks[a] for a, _ in sides]).astype(F32)
    right = jnp.stack([masks[b] for _, b in sides]).astype(F32)
    total = jnp.sum(left[:, :, None] * right[:, None], axis=-1)
    inv = (1.0 / jnp.maximum(total, 1.0)).reshape(-1)
    Y[1], D[0], U[0] = tie((Y[1], D[0], U[0]))
    Y[1], own[2], inv, scale = tie((Y[1], own[2], inv, scale))

    below, above = for_down(1), for_up(1)
    below, above, scale, D[0], U[0] = tie((below, above, scale, D[0], U[0]))
    D[1], U[1] = send(below, DOWN), send(above, UP)
    Y[2] = send(own[2], CROSS)
    far = [scale] + [send(scale, chan_route(-o)) for o in (1, 3, 4)]
    Y[2], D[1], U[1] = tie((Y[2], D[1], U[1]))
    Y[2], own[3], far = tie((Y[2], own[3], far))

    below, above = for_down(2), for_up(2)
    below, above, far, D[1], U[1] = tie((below, above, far, D[1], U[1]))
    D[2], U[2] = send(below, DOWN), send(above, UP)
    Y[3] = send(own[3], CROSS)
    scales = gather_core(gather_x(jnp.stack(far), x), core)
    out = None

    def pairs(i, base, n, offsets, side, others):
        nonlocal out
        out, res[i] = pairs_of(
            base, n, offsets, side, inv, scales, spectra, others, out
        )

    def whole(i):
        three = ((D[i], 0), (Y[i], 0), (U[i], 0))
        pairs(i, i * count, count, (0, 1, 4, 3), 5, three)

    whole(0)
    R[0] = send(res[0], NEXT)
    Y[3], D[2], U[2] = tie((Y[3], D[2], U[2]))
    Y[3], scales, out = tie((Y[3], scales, out))

    def whitened(block):
        return (block.astype(F32) * scales[1].astype(F32)).astype(BF16)

    below = for_down(3)
    below, D[2], U[2], scales = tie((below, D[2], U[2], scales))
    half = count // 2
    last = 3 * count
    first, second = send(below[:half], DOWN), send(below[half:], DOWN)
    whole(1)
    R[1] = send(res[1], NEXT)
    whole(2)
    R[2] = send(res[2], NEXT)
    first, R[0], out = tie((first, R[0], out))

    beyond = send(whitened(first), chan_route(-1))
    pairs(3, last, half, (0, 1, 4), 6, ((first, 0), (Y[3], 0)))
    R[3] = send(res[3], NEXT)
    second, out = tie((second, out))
    beyond2 = send(whitened(second), chan_route(-1))
    pairs(4, last + half, half, (0, 1, 4), 6, ((second, 0), (Y[3], half)))
    R[4] = send(res[4], NEXT)
    for i in (0, 1):
        out = placed(i * count, 2, R[i], out)
    out = last_of(last, inv, scales, spectra, beyond, ((2 * count, 2),), (R[2],), out)
    return last_of(
        last + half,
        inv,
        scales,
        spectra,
        beyond2,
        ((last, 3), (last + half, 3)),
        (R[3], R[4]),
        out,
    )


def solution(mesh):
    return jax.shard_map(
        shards,
        mesh=mesh,
        in_specs=(P("bin", None, None, "chan"), P("chan", None)),
        out_specs=P("chan", None, "bin", None, None, None),
        check_vma=False,
    )
```
